32 devices in a mesh: space: 4 (over y, core), tm: 8 (over z, x).
Axes of the slice: x: 2, y: 2, z: 4, core: 2. Of those that a mesh axis runs over, the one named last changes fastest.
Arguments:
- snapshots: bfloat16 [4096, 8192], P('space', 'tm'), may hold values from -6 to 6
- basis: bfloat16 [4096, 64], P('space'), may hold values from -0.09375 to 0.09375
- lengths: int32 [4], replicated, may hold values from 1540 to 2048
Outputs:
- gram_matrix: float32 [2144, 2144], P('space')
- right_sides: float32 [2144, 64], P('space')
The draws below stay inside these ranges and needn't reach their ends.
Inputs may be any that keep to these rules, and one draw needn't show every extreme that they name: lengths[k] snapshots of trajectory k are recorded; later positions of its slot of 2048 are padding.
All inputs are finite; a program needn't handle non-finite values.
Results may differ from the reference program's by a relative error of at most 0.0003.
Values sent between devices are 32-bit elements; how exact they have to be, the bound alone decides.
A program may use at most 64 MiB of HBM per device.

```python
import jax
import jax.numpy as jnp
import numpy as np
from jax import lax

R = 64
CELLS = 4096
T_DEV = 1024
TIMES = 8192
SLOT = 2048
TRAJ = 4


def with_ends(values, own_key, least, high):
    spot = [jax.random.randint(jax.random.fold_in(own_key, axis), (), 0, length) for axis, length in enumerate(values.shape)]
    longest = values.shape.index(max(values.shape))
    beside = spot[:longest] + [(spot[longest] + 1) % values.shape[longest]] + spot[longest + 1:]
    return values.at[tuple(spot)].set(least).at[tuple(beside)].set(high)


def steps_of(stream_key, shape, shards, least, top_value):
    level, own = 1.0, jax.random.fold_in(stream_key, 6)
    for dim, parts in shards:
        heights = jnp.exp(jax.random.uniform(jax.random.fold_in(own, dim), (parts,), jnp.float32, least / len(shards), top_value / len(shards)))
        level = level * jnp.repeat(heights, shape[dim] // parts).reshape([-1 if axis == dim else 1 for axis in range(len(shape))])
    return level


def normal_values(own_key, dims, scale, reach, shards=(), kind=jnp.bfloat16):
    values = scale * jax.random.normal(own_key, dims, jnp.float32)
    if shards:
        values = values * steps_of(own_key, dims, shards, -0.22, 0.18)
    return jnp.clip(values, -reach, reach).astype(kind)


def setup_inputs(seed: int = 0) -> dict:
    key_list = jax.random.split(jax.random.key(seed), 4)
    return {
        "snapshots": normal_values(key_list[0], (CELLS, TIMES), 1.0, 6.0, ((0, 4), (1, 8))),
        "basis": normal_values(key_list[1], (CELLS, R), CELLS ** -0.5, 0.09375, ((0, 4),)),
        "lengths": with_ends(jax.random.randint(key_list[2], (TRAJ,), T_DEV + T_DEV // 2 + 4, 2 * T_DEV + 1), jax.random.fold_in(key_list[2], 1), T_DEV + T_DEV // 2 + 4, 2 * T_DEV).astype(jnp.int32),
    }


EXACT = lax.Precision.HIGHEST

def features(block_rows):
    firsts, seconds = np.triu_indices(R)
    return jnp.concatenate([block_rows, block_rows[:, firsts] * block_rows[:, seconds]], axis=1)

def reference(snapshots, basis, lengths):
    states = jnp.dot(basis.T, snapshots, preferred_element_type=jnp.float32)
    horizon = states.shape[1]
    padded = jnp.pad(states, ((0, 0), (2, 2)))
    change = (padded[:, :horizon] - 8.0 * padded[:, 1:horizon + 1] + 8.0 * padded[:, 3:horizon + 3] - padded[:, 4:]) / 12.0
    shifted = jnp.arange(horizon, dtype=jnp.int32) + T_DEV // 2
    owners = (shifted // SLOT % lengths.shape[0]).astype(jnp.int32)
    offset = shifted % SLOT
    limits = lengths[owners]
    living = ((offset >= 2) & (offset <= limits - 3)).astype(jnp.float32)
    samples = jnp.sum(lengths - 4).astype(jnp.float32)
    masked = states * living[None, :]
    dmasked = change * living[None, :]
    energy = lax.optimization_barrier(jnp.sum(masked * masked, axis=1))
    scales = jnp.sqrt(energy / samples + 1e-06)
    scaled = (masked / scales[:, None]).T
    dscaled = (dmasked / scales[:, None]).T

    def step(totals, blocks):
        block_rows, block_change = blocks
        design = features(block_rows)
        gram_sum = totals[0] + jnp.dot(design.T, design, precision=EXACT, preferred_element_type=jnp.float32)
        side_sum = totals[1] + jnp.dot(design.T, block_change, precision=EXACT, preferred_element_type=jnp.float32)
        return ((gram_sum, side_sum), None)
    width_all = R * (R + 3) // 2
    initial = (jnp.zeros((width_all, width_all), jnp.float32), jnp.zeros((width_all, R), jnp.float32))
    pieces = horizon // T_DEV
    (gram_sum, side_sum), _ = lax.scan(step, initial, (scaled.reshape(pieces, T_DEV, R), dscaled.reshape(pieces, T_DEV, R)))
    return (gram_sum / samples, side_sum / samples)
```

```python
import functools

import jax
import jax.numpy as jnp
from jax import lax
from jax.experimental import pallas as pl
from jax.experimental.pallas import tpu as pltpu
from jax.sharding import PartitionSpec as P

LANES = 128
BF16 = jnp.bfloat16
NT = (((1,), (1,)), ((), ()))


def round_up(value, step):
    return -(-value // step) * step


def split(value):
    high = value.astype(BF16)
    return high, (value - high.astype(jnp.float32)).astype(BF16)


def gram_kernel(
    rows, feats, side_at, inv_ref, x_ref, d_ref, gram_ref, side_ref, wide, high, low, row_high, row_low, total
):
    step = pl.program_id(0)
    tiles, modes, _ = x_ref.shape
    start = lax.axis_index("space") * rows
    padded_rows = row_high.shape[0]
    width = high.shape[0]

    @pl.when(step == 0)
    def _():
        total[...] = jnp.zeros_like(total)
        wide[feats:side_at, :] = jnp.zeros((side_at - feats, LANES), jnp.float32)

    for k in range(tiles):
        lanes = slice(k * LANES, (k + 1) * LANES)
        wide[0:modes, :] = x_ref[k]
        at = modes
        for i in range(modes):
            wide[at : at + modes - i, :] = x_ref[k, i : i + 1, :] * x_ref[k, i:modes, :]
            at += modes - i
        wide[side_at:width, :] = d_ref[k]
        high[:, lanes], low[:, lanes] = split(wide[...])
        row_high[:, lanes], row_low[:, lanes] = split(wide[pl.ds(start, padded_rows), :])

    for at in range(0, width, 256):
        cols = slice(at, min(at + 256, width))
        dot = functools.partial(lax.dot_general, dimension_numbers=NT, preferred_element_type=jnp.float32)
        total[:, cols] += (
            dot(row_high[...], high[cols, :])
            + dot(row_high[...], low[cols, :])
            + dot(row_low[...], high[cols, :])
        )

    @pl.when(step == pl.num_programs(0) - 1)
    def _():
        inv = inv_ref[0]
        gram_ref[...] = total[0:rows, 0:feats] * inv
        side_ref[...] = total[0:rows, side_at:width] * inv


def gram(scaled, dscaled, inv_samples, rows, feats):
    tiles, modes, _ = scaled.shape
    per_step = 8
    side_at = round_up(feats, LANES)
    width = side_at + modes
    padded = round_up(rows, 16)
    block = pl.BlockSpec((per_step, modes, LANES), lambda t: (t, 0, 0))
    span = per_step * LANES
    return pl.pallas_call(
        functools.partial(gram_kernel, rows, feats, side_at),
        grid=(tiles // per_step,),
        in_specs=[pl.BlockSpec(memory_space=pltpu.SMEM), block, block],
        out_specs=[
            pl.BlockSpec((rows, feats), lambda t: (0, 0)),
            pl.BlockSpec((rows, modes), lambda t: (0, 0)),
        ],
        out_shape=[
            jax.ShapeDtypeStruct((rows, feats), jnp.float32),
            jax.ShapeDtypeStruct((rows, modes), jnp.float32),
        ],
        scratch_shapes=[
            pltpu.VMEM((width, LANES), jnp.float32),
            pltpu.VMEM((width, span), BF16),
            pltpu.VMEM((width, span), BF16),
            pltpu.VMEM((padded, span), BF16),
            pltpu.VMEM((padded, span), BF16),
            pltpu.VMEM((padded, width), jnp.float32),
        ],
        compiler_params=pltpu.CompilerParams(vmem_limit_bytes=56 * 1024 * 1024),
        cost_estimate=pl.CostEstimate(
            flops=6 * rows * width * tiles * LANES, bytes_accessed=4 * rows * feats, transcendentals=0
        ),
    )(inv_samples.reshape(1), scaled, dscaled)


def shards(snapshots, basis, lengths):
    modes = basis.shape[1]
    feats = modes * (modes + 3) // 2
    horizon = snapshots.shape[1]
    rows = feats // lax.axis_size("space")
    partial = jnp.einsum("cr,ct->rt", basis, snapshots, preferred_element_type=jnp.float32)
    partial = partial.reshape(modes, horizon // LANES, LANES).transpose(1, 0, 2)
    share = lax.psum_scatter(partial, "space", scatter_dimension=0, tiled=True)
    states = lax.all_gather(share, ("tm", "space"), axis=0, tiled=True)
    tiles = states.shape[0]

    before = jnp.pad(states[:-1, :, -2:], ((1, 0), (0, 0), (0, 0)))
    after = jnp.pad(states[1:, :, :2], ((0, 1), (0, 0), (0, 0)))
    wide = jnp.concatenate([before, states, after], axis=2)
    change = (
        wide[:, :, :LANES]
        - 8.0 * wide[:, :, 1 : LANES + 1]
        + 8.0 * wide[:, :, 3 : LANES + 3]
        - wide[:, :, 4:]
    ) / 12.0

    slot = 2 * horizon
    shifted = jnp.arange(tiles * LANES, dtype=jnp.int32) + horizon // 2
    offsets = shifted % slot
    owners = shifted // slot % lengths.shape[0]
    match = owners[:, None] == jnp.arange(lengths.shape[0], dtype=jnp.int32)[None, :]
    limits = jnp.sum(jnp.where(match, lengths[None, :], 0), axis=1)
    living = ((offsets >= 2) & (offsets <= limits - 3)).astype(jnp.float32).reshape(tiles, 1, LANES)
    samples = jnp.sum(lengths - 4).astype(jnp.float32)
    masked = states * living
    energy = jnp.sum(masked * masked, axis=(0, 2))
    inverse = (1.0 / jnp.sqrt(energy / samples + 1e-06))[None, :, None]
    return tuple(gram(masked * inverse, change * living * inverse, 1.0 / samples, rows, feats))


def solution(mesh):
    return jax.shard_map(
        shards,
        mesh=mesh,
        in_specs=(P("space", "tm"), P("space", None), P()),
        out_specs=(P("space", None), P("space", None)),
        check_vma=False,
    )
```

```python
import functools

import jax
import jax.numpy as jnp
from jax import lax
from jax.experimental import pallas as pl
from jax.experimental.pallas import tpu as pltpu
from jax.sharding import PartitionSpec as P

LANES = 128
BF16 = jnp.bfloat16
F8 = jnp.float8_e5m2
LIFT = 256.0
NT = (((1,), (1,)), ((), ()))


def round_up(value, step):
    return -(-value // step) * step


def split(value):
    high = value.astype(BF16)
    return high, value - high.astype(jnp.float32)


def gather_kernel(part_ref, out_ref, landing, rs_send, rs_recv, tm_send, tm_recv, par_send, par_recv, sib_send, sib_recv):
    spaces, times = lax.axis_size("space"), lax.axis_size("tm")
    s, t = lax.axis_index("space"), lax.axis_index("tm")
    per = landing.shape[1]
    pairs = spaces // 2
    sibling = s + 1 - 2 * lax.rem(s, 2)

    def around(value, step, count):
        return lax.rem(value + step + count, count)

    def block(owner_t, owner_s):
        return out_ref.at[owner_t * spaces + owner_s]

    def remote(src, dst, send, recv, to_s, to_t):
        return pltpu.make_async_remote_copy(
            src_ref=src,
            dst_ref=dst,
            send_sem=send,
            recv_sem=recv,
            device_id=(to_s, to_t),
            device_id_type=pl.DeviceIdType.MESH,
        )

    barrier = pltpu.get_barrier_semaphore()
    for d in range(1, spaces):
        pl.semaphore_signal(
            barrier, inc=1, device_id=(around(s, d, spaces), t), device_id_type=pl.DeviceIdType.MESH
        )
    for d in range(1, times):
        pl.semaphore_signal(
            barrier, inc=1, device_id=(s, around(t, d, times)), device_id_type=pl.DeviceIdType.MESH
        )
    pl.semaphore_wait(barrier, spaces + times - 2)

    sent = []
    first = []
    for d in range(1, spaces):
        to = around(s, d, spaces)
        copy = remote(part_ref.at[pl.ds(to * per, per)], landing.at[d - 1], rs_send.at[d - 1], rs_recv.at[d - 1], to, t)
        copy.start()
        first.append(copy)
    own = part_ref[pl.ds(s * per, per)]
    for d in range(1, spaces):
        first[d - 1].wait_recv()
        own = own + landing[d - 1]
    sent += first
    out_ref[t * spaces + s] = own

    across = []
    for d in range(1, times):
        copy = remote(block(t, s), block(t, s), tm_send.at[d - 1], tm_recv.at[d - 1], s, around(t, d, times))
        copy.start()
        across.append(copy)
    sent += across

    beside = {}
    twins = []
    for d in range(times + 1):
        if d < times:
            src_t = around(t, -d, times)
            if d > 0:
                across[d - 1].wait_recv()
            here = block(src_t, s)
            for e in range(1, pairs):
                at = d * (pairs - 1) + e - 1
                copy = remote(here, here, par_send.at[at], par_recv.at[at], around(s, 2 * e, spaces), t)
                copy.start()
                beside[d, e] = copy
            copy = remote(here, here, sib_send.at[d * pairs], sib_recv.at[d * pairs], sibling, t)
            copy.start()
            twins.append(copy)
        if d > 0:
            src_t = around(t, 1 - d, times)
            for e in range(1, pairs):
                beside[d - 1, e].wait_recv()
                there = block(src_t, around(s, -2 * e, spaces))
                at = (d - 1) * pairs + e
                copy = remote(there, there, sib_send.at[at], sib_recv.at[at], sibling, t)
                copy.start()
                twins.append(copy)
    for copy in twins:
        copy.wait_recv()
    for copy in sent + list(beside.values()) + twins:
        copy.wait_send()


def gathered(part):
    spaces, times = lax.axis_size("space"), lax.axis_size("tm")
    tiles, modes, lanes = part.shape
    per = tiles // spaces
    pairs = spaces // 2
    dma = pltpu.SemaphoreType.DMA
    out = pl.pallas_call(
        gather_kernel,
        in_specs=[pl.BlockSpec(memory_space=pltpu.VMEM)],
        out_specs=pl.BlockSpec(memory_space=pltpu.VMEM),
        out_shape=jax.ShapeDtypeStruct((times * spaces, per, modes, lanes), jnp.float32),
        scratch_shapes=[
            pltpu.VMEM((spaces - 1, per, modes, lanes), jnp.float32),
            dma((spaces - 1,)),
            dma((spaces - 1,)),
            dma((times - 1,)),
            dma((times - 1,)),
            dma((max(1, times * (pairs - 1)),)),
            dma((max(1, times * (pairs - 1)),)),
            dma((times * pairs,)),
            dma((times * pairs,)),
        ],
        compiler_params=pltpu.CompilerParams(
            collective_id=0, has_side_effects=True, vmem_limit_bytes=32 * 1024 * 1024
        ),
    )(part)
    return out.reshape(times * tiles, modes, lanes)


def gram_kernel(
    rows, feats, side_at, inv_ref, x_ref, live_ref, gram_ref, side_ref,
    inverse, scaled, wide, high, low, high8, low8, row_high, row_low, row_high8, row_low8, total
):
    step = pl.program_id(0)
    count, modes, _ = x_ref.shape
    tiles = high.shape[1] // LANES
    start = lax.axis_index("space") * rows
    padded_rows = row_high.shape[0]
    width = high.shape[0]
    whole = high8.shape[0]
    lane = lax.broadcasted_iota(jnp.int32, (modes, LANES), 1)

    @pl.when(step == 0)
    def _():
        total[...] = jnp.zeros_like(total)
        wide[feats:side_at, :] = jnp.zeros((side_at - feats, LANES), jnp.float32)

        def add(k, energy):
            masked = x_ref[k] * live_ref[k]
            return energy + masked * masked

        energy = lax.fori_loop(0, count, add, jnp.zeros((modes, LANES), jnp.float32), unroll=8)
        energy = jnp.sum(energy, axis=1, keepdims=True) * inv_ref[0]
        inverse[...] = jnp.broadcast_to(1.0 / jnp.sqrt(energy + 1e-06), (modes, LANES))

    for k in range(tiles):
        at = step * tiles + k
        lanes = slice(k * LANES, (k + 1) * LANES)
        x = x_ref[at]
        weight = inverse[...] * live_ref[at]
        prev = x_ref[jnp.maximum(at - 1, 0)] * (at > 0).astype(jnp.float32)
        after = x_ref[jnp.minimum(at + 1, count - 1)] * (at < count - 1).astype(jnp.float32)
        back2 = pltpu.roll(jnp.where(lane >= LANES - 2, prev, x), 2, 1)
        back1 = pltpu.roll(jnp.where(lane >= LANES - 1, prev, x), 1, 1)
        ahead1 = pltpu.roll(jnp.where(lane < 1, after, x), LANES - 1, 1)
        ahead2 = pltpu.roll(jnp.where(lane < 2, after, x), LANES - 2, 1)
        change = (back2 - 8.0 * back1 + 8.0 * ahead1 - ahead2) * (1.0 / 12.0)
        scaled[k] = x * weight
        wide[0:modes, :] = x * weight
        wide[side_at:width, :] = change * weight
        at = modes
        for i in range(modes):
            wide[at : at + modes - i, :] = scaled[k, i : i + 1, :] * scaled[k, i:modes, :]
            at += modes - i
        value = wide[...]
        high[:, lanes], rest = split(value)
        low[whole:width, lanes] = rest[whole:width].astype(BF16)
        high8[:, lanes] = value[0:whole].astype(F8)
        low8[:, lanes] = (rest[0:whole] * LIFT).astype(F8)
        value = wide[pl.ds(start, padded_rows), :]
        row_high[:, lanes], rest = split(value)
        row_low[:, lanes] = rest.astype(BF16)
        row_high8[:, lanes] = value.astype(F8)
        row_low8[:, lanes] = (rest * LIFT).astype(F8)

    dot = functools.partial(lax.dot_general, dimension_numbers=NT, preferred_element_type=jnp.float32)
    for at in range(0, whole, 256):
        cols = slice(at, at + 256)
        total[:, cols] += dot(row_high[...], high[cols, :]) + (1.0 / LIFT) * (
            dot(row_high8[...], low8[cols, :]) + dot(row_low8[...], high8[cols, :])
        )
    cols = slice(whole, width)
    total[:, cols] += (
        dot(row_high[...], high[cols, :]) + dot(row_high[...], low[cols, :]) + dot(row_low[...], high[cols, :])
    )

    @pl.when(step == pl.num_programs(0) - 1)
    def _():
        inv = inv_ref[0]
        gram_ref[...] = total[0:rows, 0:feats] * inv
        side_ref[...] = total[0:rows, side_at:width] * inv


def gram(states, living, inv_samples, rows, feats):
    tiles, modes, _ = states.shape
    per_step = 8
    side_at = round_up(feats, LANES)
    width = side_at + modes
    whole = feats // 256 * 256
    padded = round_up(rows, 32)
    span = per_step * LANES
    vmem = pl.BlockSpec(memory_space=pltpu.VMEM)
    return pl.pallas_call(
        functools.partial(gram_kernel, rows, feats, side_at),
        grid=(tiles // per_step,),
        in_specs=[pl.BlockSpec(memory_space=pltpu.SMEM), vmem, vmem],
        out_specs=[
            pl.BlockSpec((rows, feats), lambda t: (0, 0)),
            pl.BlockSpec((rows, modes), lambda t: (0, 0)),
        ],
        out_shape=[
            jax.ShapeDtypeStruct((rows, feats), jnp.float32),
            jax.ShapeDtypeStruct((rows, modes), jnp.float32),
        ],
        scratch_shapes=[
            pltpu.VMEM((modes, LANES), jnp.float32),
            pltpu.VMEM((per_step, modes, LANES), jnp.float32),
            pltpu.VMEM((width, LANES), jnp.float32),
            pltpu.VMEM((width, span), BF16),
            pltpu.VMEM((width, span), BF16),
            pltpu.VMEM((whole, span), F8),
            pltpu.VMEM((whole, span), F8),
            pltpu.VMEM((padded, span), BF16),
            pltpu.VMEM((padded, span), BF16),
            pltpu.VMEM((padded, span), F8),
            pltpu.VMEM((padded, span), F8),
            pltpu.VMEM((padded, width), jnp.float32),
        ],
        compiler_params=pltpu.CompilerParams(vmem_limit_bytes=56 * 1024 * 1024),
        cost_estimate=pl.CostEstimate(
            flops=6 * rows * width * tiles * LANES, bytes_accessed=4 * rows * feats, transcendentals=0
        ),
    )(inv_samples.reshape(1), states, living)


def shards(snapshots, basis, lengths):
    modes = basis.shape[1]
    feats = modes * (modes + 3) // 2
    horizon = snapshots.shape[1]
    rows = feats // lax.axis_size("space")
    partial = jnp.einsum("cr,ct->rt", basis, snapshots, preferred_element_type=jnp.float32)
    partial = partial.reshape(modes, horizon // LANES, LANES).transpose(1, 0, 2)
    states = gathered(partial)
    tiles = states.shape[0]

    slot = 2 * horizon
    shifted = jnp.arange(tiles * LANES, dtype=jnp.int32) + horizon // 2
    offsets = shifted % slot
    owners = shifted // slot % lengths.shape[0]
    match = owners[:, None] == jnp.arange(lengths.shape[0], dtype=jnp.int32)[None, :]
    limits = jnp.sum(jnp.where(match, lengths[None, :], 0), axis=1)
    living = ((offsets >= 2) & (offsets <= limits - 3)).astype(jnp.float32).reshape(tiles, 1, LANES)
    samples = jnp.sum(lengths - 4).astype(jnp.float32)
    return tuple(gram(states, living, 1.0 / samples, rows, feats))


def solution(mesh):
    return jax.shard_map(
        shards,
        mesh=mesh,
        in_specs=(P("space", "tm"), P("space", None), P()),
        out_specs=(P("space", None), P("space", None)),
        check_vma=False,
    )
```

```python
import functools

import jax
import jax.numpy as jnp
from jax import lax
from jax.experimental import pallas as pl
from jax.experimental.pallas import tpu as pltpu
from jax.sharding import PartitionSpec as P

LANES = 128
BF16 = jnp.bfloat16
F8 = jnp.float8_e5m2
LIFT = 256.0
NT = (((1,), (1,)), ((), ()))


def round_up(value, step):
    return -(-value // step) * step


def split(value):
    high = value.astype(BF16)
    return high, value - high.astype(jnp.float32)


def gather_kernel(part_ref, out_ref, landing, rs_send, rs_recv, tm_send, tm_recv, par_send, par_recv, sib_send, sib_recv):
    spaces, times = lax.axis_size("space"), lax.axis_size("tm")
    s, t = lax.axis_index("space"), lax.axis_index("tm")
    per = landing.shape[1]
    pairs = spaces // 2
    sibling = s + 1 - 2 * lax.rem(s, 2)

    def around(value, step, count):
        return lax.rem(value + step + count, count)

    def block(owner_t, owner_s):
        return out_ref.at[owner_t * spaces + owner_s]

    def remote(src, dst, send, recv, to_s, to_t):
        return pltpu.make_async_remote_copy(
            src_ref=src,
            dst_ref=dst,
            send_sem=send,
            recv_sem=recv,
            device_id=(to_s, to_t),
            device_id_type=pl.DeviceIdType.MESH,
        )

    barrier = pltpu.get_barrier_semaphore()
    for d in range(1, spaces):
        pl.semaphore_signal(
            barrier, inc=1, device_id=(around(s, d, spaces), t), device_id_type=pl.DeviceIdType.MESH
        )
    for d in range(1, times):
        pl.semaphore_signal(
            barrier, inc=1, device_id=(s, around(t, d, times)), device_id_type=pl.DeviceIdType.MESH
        )
    pl.semaphore_wait(barrier, spaces + times - 2)

    sent = []
    first = []
    for d in range(1, spaces):
        to = around(s, d, spaces)
        copy = remote(part_ref.at[pl.ds(to * per, per)], landing.at[d - 1], rs_send.at[d - 1], rs_recv.at[d - 1], to, t)
        copy.start()
        first.append(copy)
    own = part_ref[pl.ds(s * per, per)]
    for d in range(1, spaces):
        first[d - 1].wait_recv()
        own = own + landing[d - 1]
    sent += first
    out_ref[t * spaces + s] = own

    across = []
    for d in range(1, times):
        copy = remote(block(t, s), block(t, s), tm_send.at[d - 1], tm_recv.at[d - 1], s, around(t, d, times))
        copy.start()
        across.append(copy)
    sent += across

    beside = {}
    twins = []
    for d in range(times + 1):
        if d < times:
            src_t = around(t, -d, times)
            if d > 0:
                across[d - 1].wait_recv()
            here = block(src_t, s)
            for e in range(1, pairs):
                at = d * (pairs - 1) + e - 1
                copy = remote(here, here, par_send.at[at], par_recv.at[at], around(s, 2 * e, spaces), t)
                copy.start()
                beside[d, e] = copy
            copy = remote(here, here, sib_send.at[d * pairs], sib_recv.at[d * pairs], sibling, t)
            copy.start()
            twins.append(copy)
        if d > 0:
            src_t = around(t, 1 - d, times)
            for e in range(1, pairs):
                beside[d - 1, e].wait_recv()
                there = block(src_t, around(s, -2 * e, spaces))
                at = (d - 1) * pairs + e
                copy = remote(there, there, sib_send.at[at], sib_recv.at[at], sibling, t)
                copy.start()
                twins.append(copy)
    for copy in twins:
        copy.wait_recv()
    for copy in sent + list(beside.values()) + twins:
        copy.wait_send()


def gathered(part):
    spaces, times = lax.axis_size("space"), lax.axis_size("tm")
    tiles, modes, lanes = part.shape
    per = tiles // spaces
    pairs = spaces // 2
    dma = pltpu.SemaphoreType.DMA
    out = pl.pallas_call(
        gather_kernel,
        in_specs=[pl.BlockSpec(memory_space=pltpu.VMEM)],
        out_specs=pl.BlockSpec(memory_space=pltpu.VMEM),
        out_shape=jax.ShapeDtypeStruct((times * spaces, per, modes, lanes), jnp.float32),
        scratch_shapes=[
            pltpu.VMEM((spaces - 1, per, modes, lanes), jnp.float32),
            dma((spaces - 1,)),
            dma((spaces - 1,)),
            dma((times - 1,)),
            dma((times - 1,)),
            dma((max(1, times * (pairs - 1)),)),
            dma((max(1, times * (pairs - 1)),)),
            dma((times * pairs,)),
            dma((times * pairs,)),
        ],
        compiler_params=pltpu.CompilerParams(
            collective_id=0, has_side_effects=True, vmem_limit_bytes=32 * 1024 * 1024
        ),
    )(part)
    return out.reshape(times * tiles, modes, lanes)


def gram_kernel(
    rows, feats, side_at, horizon, lengths_ref, x_ref, gram_ref, side_ref,
    inverse, scaled, wide, high, low, high8, low8, row_high, row_low, row_high8, row_low8, total
):
    step = pl.program_id(0)
    count, modes, _ = x_ref.shape
    tiles = high.shape[1] // LANES
    start = lax.axis_index("space") * rows
    padded_rows = row_high.shape[0]
    width = high.shape[0]
    whole = high8.shape[0]
    lane = lax.broadcasted_iota(jnp.int32, (modes, LANES), 1)

    trajectories = lengths_ref.shape[0]
    samples = lengths_ref[0] - 4
    for k in range(1, trajectories):
        samples = samples + lengths_ref[k] - 4
    inv = 1.0 / jnp.full((1, 1), samples.astype(jnp.float32))

    def living(at):
        shifted = at * LANES + horizon // 2
        limit = lengths_ref[lax.rem(lax.div(shifted, 2 * horizon), trajectories)]
        offset = lax.rem(shifted, 2 * horizon) + lane
        return ((offset >= 2) & (offset <= limit - 3)).astype(jnp.float32)

    @pl.when(step == 0)
    def _():
        total[...] = jnp.zeros_like(total)
        wide[feats:side_at, :] = jnp.zeros((side_at - feats, LANES), jnp.float32)

        def add(k, energy):
            masked = x_ref[k] * living(k)
            return energy + masked * masked

        energy = lax.fori_loop(0, count, add, jnp.zeros((modes, LANES), jnp.float32), unroll=8)
        energy = jnp.sum(energy, axis=1, keepdims=True) * inv
        inverse[...] = jnp.broadcast_to(1.0 / jnp.sqrt(energy + 1e-06), (modes, LANES))

    for k in range(tiles):
        at = step * tiles + k
        lanes = slice(k * LANES, (k + 1) * LANES)
        x = x_ref[at]
        weight = inverse[...] * living(at)
        prev = x_ref[jnp.maximum(at - 1, 0)] * (at > 0).astype(jnp.float32)
        after = x_ref[jnp.minimum(at + 1, count - 1)] * (at < count - 1).astype(jnp.float32)
        back2 = pltpu.roll(jnp.where(lane >= LANES - 2, prev, x), 2, 1)
        back1 = pltpu.roll(jnp.where(lane >= LANES - 1, prev, x), 1, 1)
        ahead1 = pltpu.roll(jnp.where(lane < 1, after, x), LANES - 1, 1)
        ahead2 = pltpu.roll(jnp.where(lane < 2, after, x), LANES - 2, 1)
        change = (back2 - 8.0 * back1 + 8.0 * ahead1 - ahead2) * (1.0 / 12.0)
        scaled[k] = x * weight
        wide[0:modes, :] = x * weight
        wide[side_at:width, :] = change * weight
        at = modes
        for i in range(modes):
            wide[at : at + modes - i, :] = scaled[k, i : i + 1, :] * scaled[k, i:modes, :]
            at += modes - i
        value = wide[...]
        high[:, lanes], rest = split(value)
        low[:, lanes] = rest[whole:width].astype(BF16)
        high8[:, lanes] = value[0:whole].astype(F8)
        low8[:, lanes] = (rest[0:whole] * LIFT).astype(F8)
        value = wide[pl.ds(start, padded_rows), :]
        row_high[:, lanes], rest = split(value)
        row_low[:, lanes] = rest.astype(BF16)
        row_high8[:, lanes] = value.astype(F8)
        row_low8[:, lanes] = (rest * LIFT).astype(F8)

    dot = functools.partial(lax.dot_general, dimension_numbers=NT, preferred_element_type=jnp.float32)
    for at in range(0, whole, 256):
        cols = slice(at, at + 256)
        total[:, cols] += dot(row_high[...], high[cols, :]) + (1.0 / LIFT) * (
            dot(row_high8[...], low8[cols, :]) + dot(row_low8[...], high8[cols, :])
        )
    cols = slice(whole, width)
    total[:, cols] += (
        dot(row_high[...], high[cols, :]) + dot(row_high[...], low[...]) + dot(row_low[...], high[cols, :])
    )

    @pl.when(step == pl.num_programs(0) - 1)
    def _():
        gram_ref[...] = total[0:rows, 0:feats] * inv
        side_ref[...] = total[0:rows, side_at:width] * inv


def gram(states, lengths, horizon, rows, feats):
    tiles, modes, _ = states.shape
    per_step = 16
    side_at = round_up(feats, LANES)
    width = side_at + modes
    whole = feats // 256 * 256
    padded = round_up(rows, 32)
    span = per_step * LANES
    vmem = pl.BlockSpec(memory_space=pltpu.VMEM)
    return pl.pallas_call(
        functools.partial(gram_kernel, rows, feats, side_at, horizon),
        grid=(tiles // per_step,),
        in_specs=[pl.BlockSpec(memory_space=pltpu.SMEM), vmem],
        out_specs=[
            pl.BlockSpec((rows, feats), lambda t: (0, 0)),
            pl.BlockSpec((rows, modes), lambda t: (0, 0)),
        ],
        out_shape=[
            jax.ShapeDtypeStruct((rows, feats), jnp.float32),
            jax.ShapeDtypeStruct((rows, modes), jnp.float32),
        ],
        scratch_shapes=[
            pltpu.VMEM((modes, LANES), jnp.float32),
            pltpu.VMEM((per_step, modes, LANES), jnp.float32),
            pltpu.VMEM((width, LANES), jnp.float32),
            pltpu.VMEM((width, span), BF16),
            pltpu.VMEM((width - whole, span), BF16),
            pltpu.VMEM((whole, span), F8),
            pltpu.VMEM((whole, span), F8),
            pltpu.VMEM((padded, span), BF16),
            pltpu.VMEM((padded, span), BF16),
            pltpu.VMEM((padded, span), F8),
            pltpu.VMEM((padded, span), F8),
            pltpu.VMEM((padded, width), jnp.float32),
        ],
        compiler_params=pltpu.CompilerParams(vmem_limit_bytes=56 * 1024 * 1024),
        cost_estimate=pl.CostEstimate(
            flops=6 * rows * width * tiles * LANES, bytes_accessed=4 * rows * feats, transcendentals=0
        ),
    )(lengths, states)


def shards(snapshots, basis, lengths):
    modes = basis.shape[1]
    feats = modes * (modes + 3) // 2
    horizon = snapshots.shape[1]
    rows = feats // lax.axis_size("space")
    partial = jnp.einsum("cr,ct->rt", basis, snapshots, preferred_element_type=jnp.float32)
    partial = partial.reshape(modes, horizon // LANES, LANES).transpose(1, 0, 2)
    states = gathered(partial)
    return tuple(gram(states, lengths, horizon, rows, feats))


def solution(mesh):
    return jax.shard_map(
        shards,
        mesh=mesh,
        in_specs=(P("space", "tm"), P("space", None), P()),
        out_specs=(P("space", None), P("space", None)),
        check_vma=False,
    )
```
